32 devices in a mesh: seq: 8 (over y, x, core), mlp: 4 (over z).
Axes of the slice: x: 2, y: 2, z: 4, core: 2. Of those that a mesh axis runs over, the one named last changes fastest.
Arguments:
- tokens: bfloat16 [2, 4096, 2048], P(None, ('seq', 'mlp')), may hold values from -6 to 6
- lengths: int32 [2], replicated, may hold values from 2048 to 4096, as said below
- cotangent: bfloat16 [2, 4096, 2048], P(None, ('seq', 'mlp')), may hold values from -6 to 6
- mixer_gain: bfloat16 [2048], replicated, may hold values from 0.5 to 1.5
- query_weight: bfloat16 [2048, 2048], P(('seq', 'mlp')), may hold values from -0.125 to 0.125
- key_matrix: bfloat16 [2048, 512], P(('seq', 'mlp')), may hold values from -0.125 to 0.125
- value_matrix: bfloat16 [2048, 512], P(('seq', 'mlp')), may hold values from -0.125 to 0.125
- out_weight: bfloat16 [2048, 2048], P(('seq', 'mlp')), may hold values from -0.375 to 0.375
- query_down: bfloat16 [2048, 8], P(('seq', 'mlp')), may hold values from -0.125 to 0.125
- query_lift: bfloat16 [8, 2048], replicated, may hold values from -2 to 2
- key_down: bfloat16 [2048, 8], P(('seq', 'mlp')), may hold values from -0.125 to 0.125
- key_adapter_second: bfloat16 [8, 512], replicated, may hold values from -2 to 2
- value_down: bfloat16 [2048, 8], P(('seq', 'mlp')), may hold values from -0.125 to 0.125
- value_adapter_second: bfloat16 [8, 512], replicated, may hold values from -2 to 2
- out_down: bfloat16 [2048, 8], P(('seq', 'mlp')), may hold values from -0.375 to 0.375
- out_lift: bfloat16 [8, 2048], replicated, may hold values from -2 to 2
- query_feature_map: bfloat16 [32, 64, 64], replicated, may hold values from -0.75 to 0.75
- key_feature_map: bfloat16 [8, 64, 64], replicated, may hold values from -0.75 to 0.75
- ffn_gain: bfloat16 [2048], replicated, may hold values from 0.5 to 1.5
- gate_weight: bfloat16 [2048, 8192], P('seq', 'mlp'), may hold values from -0.125 to 0.125
- up_weight: bfloat16 [2048, 8192], P('seq', 'mlp'), may hold values from -0.125 to 0.125
- down_weight: bfloat16 [8192, 2048], P('mlp', 'seq'), may hold values from -0.125 to 0.125
Outputs:
- layer_output: bfloat16 [2, 4096, 2048], P(None, ('seq', 'mlp'))
- tokens_gradient: float32 [2, 4096, 2048], P(None, ('seq', 'mlp'))
- mixer_gain_gradient: float32 [2048], replicated
- query_weight_gradient: float32 [2048, 2048], P(('seq', 'mlp'))
- key_weight_gradient: float32 [2048, 512], P(('seq', 'mlp'))
- value_weight_gradient: float32 [2048, 512], P(('seq', 'mlp'))
- out_weight_gradient: float32 [2048, 2048], P(('seq', 'mlp'))
- query_down_gradient: float32 [2048, 8], P(('seq', 'mlp'))
- query_lift_gradient: float32 [8, 2048], replicated
- key_down_gradient: float32 [2048, 8], P(('seq', 'mlp'))
- key_lift_gradient: float32 [8, 512], replicated
- value_down_gradient: float32 [2048, 8], P(('seq', 'mlp'))
- value_lift_gradient: float32 [8, 512], replicated
- out_down_gradient: float32 [2048, 8], P(('seq', 'mlp'))
- out_lift_gradient: float32 [8, 2048], replicated
- feature_query_gradient: float32 [32, 64, 64], replicated
- feature_key_gradient: float32 [8, 64, 64], replicated
- ffn_gain_gradient: float32 [2048], replicated
- gate_weight_gradient: float32 [2048, 8192], P('seq', 'mlp')
- up_weight_gradient: float32 [2048, 8192], P('seq', 'mlp')
- down_weight_gradient: float32 [8192, 2048], P('mlp', 'seq')
The draws below stay inside these ranges and needn't reach their ends.
Inputs may be any that keep to these rules, and one draw needn't show every extreme that they name: lengths[b] is the number of tokens of sequence b, placed at its first positions; one sequence, drawn from the seed, fills all 4096 positions.
All inputs are finite; a program needn't handle non-finite values.
Results may differ from the reference program's by a relative error of at most 0.017.
The reference program's roundings to bfloat16 on the way count: a program that leaves them out, or rounds other values in their place, can miss the bound.
Values may be sent and summed in bfloat16 or wider, within the bound.
A program may use at most 576 MiB of HBM per device.

```python
import jax
import jax.numpy as jnp
from jax import lax

MODEL_WIDTH = 2048
QUERY_HEAD_COUNT = 32
KEY_VALUE_HEADS = 8
HEAD_SIZE = 64
FF = 8192
ADAPTER_RANK = 8
WINDOW_KEYS = 64
BATCH = 2
LENGTH = 4096


def draw_lengths(key, part):
    key = jax.random.fold_in(key, 11)
    pick_key, size_key = jax.random.split(key)
    chosen = jax.random.randint(pick_key, (), 0, BATCH)
    others = jax.random.randint(size_key, (BATCH,), LENGTH // 2, LENGTH + 1)
    return jnp.where(jnp.arange(BATCH) == chosen, LENGTH, others).astype(jnp.int32)


def levels(key, shape, pieces, smallest, largest):
    level, own = 1.0, jax.random.fold_in(key, 6)
    for position, blocks in pieces:
        steps = jnp.exp(jax.random.uniform(jax.random.fold_in(own, position), (blocks,), jnp.float32, smallest / len(pieces), largest / len(pieces)))
        level = level * jnp.repeat(steps, shape[position] // blocks).reshape([-1 if axis == position else 1 for axis in range(len(shape))])
    return level


def gaussian(key, shape, spread, reach, cuts=(), kind=jnp.bfloat16):
    array = spread * jax.random.normal(key, shape, jnp.float32)
    if cuts:
        array = array * levels(key, shape, cuts, -0.22, 0.18)
    return jnp.clip(array, -reach, reach).astype(kind)


def setup_inputs(seed: int = 0) -> dict:
    keys = jax.random.split(jax.random.key(seed), 23)
    tokens = gaussian(keys[0], (BATCH, LENGTH, MODEL_WIDTH), 1.0, 6.0, ((1, 32),))
    lengths = draw_lengths(jax.random.fold_in(keys[22], 71), 0)
    cotangent = gaussian(keys[2], (BATCH, LENGTH, MODEL_WIDTH), 1.0, 6.0, ((1, 32),))
    mixer_gain = jnp.clip(1.0 + 0.1 * jax.random.normal(keys[3], (MODEL_WIDTH,), jnp.float32), 0.5, 1.5).astype(jnp.bfloat16)
    query_weight = gaussian(keys[4], (MODEL_WIDTH, QUERY_HEAD_COUNT * HEAD_SIZE), MODEL_WIDTH ** -0.5, 0.125, ((0, 32),))
    key_matrix = gaussian(keys[5], (MODEL_WIDTH, KEY_VALUE_HEADS * HEAD_SIZE), MODEL_WIDTH ** -0.5, 0.125, ((0, 32),))
    value_matrix = gaussian(keys[6], (MODEL_WIDTH, KEY_VALUE_HEADS * HEAD_SIZE), MODEL_WIDTH ** -0.5, 0.125, ((0, 32),))
    out_weight = gaussian(keys[7], (QUERY_HEAD_COUNT * HEAD_SIZE, MODEL_WIDTH), (QUERY_HEAD_COUNT * HEAD_SIZE // 8) ** -0.5, 0.375, ((0, 32),))
    query_down = gaussian(keys[8], (MODEL_WIDTH, ADAPTER_RANK), MODEL_WIDTH ** -0.5, 0.125, ((0, 32),))
    query_lift = gaussian(keys[9], (ADAPTER_RANK, QUERY_HEAD_COUNT * HEAD_SIZE), ADAPTER_RANK ** -0.5, 2.0)
    key_down = gaussian(keys[10], (MODEL_WIDTH, ADAPTER_RANK), MODEL_WIDTH ** -0.5, 0.125, ((0, 32),))
    key_adapter_second = gaussian(keys[11], (ADAPTER_RANK, KEY_VALUE_HEADS * HEAD_SIZE), ADAPTER_RANK ** -0.5, 2.0)
    value_down = gaussian(keys[12], (MODEL_WIDTH, ADAPTER_RANK), MODEL_WIDTH ** -0.5, 0.125, ((0, 32),))
    value_adapter_second = gaussian(keys[13], (ADAPTER_RANK, KEY_VALUE_HEADS * HEAD_SIZE), ADAPTER_RANK ** -0.5, 2.0)
    out_down = gaussian(keys[14], (QUERY_HEAD_COUNT * HEAD_SIZE, ADAPTER_RANK), (QUERY_HEAD_COUNT * HEAD_SIZE // 8) ** -0.5, 0.375, ((0, 32),))
    out_lift = gaussian(keys[15], (ADAPTER_RANK, MODEL_WIDTH), ADAPTER_RANK ** -0.5, 2.0)
    query_feature_map = gaussian(keys[16], (QUERY_HEAD_COUNT, HEAD_SIZE, HEAD_SIZE), HEAD_SIZE ** -0.5, 0.75)
    key_feature_map = gaussian(keys[17], (KEY_VALUE_HEADS, HEAD_SIZE, HEAD_SIZE), HEAD_SIZE ** -0.5, 0.75)
    ffn_gain = jnp.clip(1.0 + 0.1 * jax.random.normal(keys[18], (MODEL_WIDTH,), jnp.float32), 0.5, 1.5).astype(jnp.bfloat16)
    gate_weight = gaussian(keys[19], (MODEL_WIDTH, FF), MODEL_WIDTH ** -0.5, 0.125, ((0, 8), (1, 4)))
    up_weight = gaussian(keys[20], (MODEL_WIDTH, FF), MODEL_WIDTH ** -0.5, 0.125, ((0, 8), (1, 4)))
    down_weight = gaussian(keys[21], (FF, MODEL_WIDTH), (FF // 4) ** -0.5, 0.125, ((0, 4), (1, 8)))
    return {"tokens": tokens, "lengths": lengths, "cotangent": cotangent, "mixer_gain": mixer_gain, "query_weight": query_weight, "key_matrix": key_matrix, "value_matrix": value_matrix, "out_weight": out_weight, "query_down": query_down, "query_lift": query_lift, "key_down": key_down, "key_adapter_second": key_adapter_second, "value_down": value_down, "value_adapter_second": value_adapter_second, "out_down": out_down, "out_lift": out_lift, "query_feature_map": query_feature_map, "key_feature_map": key_feature_map, "ffn_gain": ffn_gain, "gate_weight": gate_weight, "up_weight": up_weight, "down_weight": down_weight}


@jax.custom_vjp
def low(v):
    return lax.optimization_barrier(v.astype(jnp.bfloat16)).astype(jnp.float32)

@jax.custom_vjp
def low_back(v):
    return v

def low_keep(v):
    return (low(v), None)

def low_pass(kept, grad):
    return (grad,)

def back_keep(v):
    return (v, None)

def back_low(kept, grad):
    return (low(grad),)
low.defvjp(low_keep, low_pass)
low_back.defvjp(back_keep, back_low)
EPSILON = 1e-05
HIGHEST = lax.Precision.HIGHEST

def matmul(left, right):
    return jnp.dot(left, right, precision=HIGHEST, preferred_element_type=jnp.float32)

def feature_map(value_block):
    return jnp.concatenate([jax.nn.softmax(value_block, axis=-1), jax.nn.softmax(-value_block, axis=-1)], axis=-1)

def mix_block(query_block_rows, key_block, value_block, state, totals, query_feature_rows, feature_k, start_index):
    token_rows = query_block_rows.shape[1]
    extent = key_block.shape[1]
    margin = extent - token_rows
    head = query_block_rows.shape[-1]
    mapped_q = feature_map(jnp.einsum('nrhgd,hgde->nrhge', query_block_rows, query_feature_rows, precision=HIGHEST))
    mapped_k = feature_map(jnp.einsum('nkhd,hde->nkhe', key_block, feature_k, precision=HIGHEST))
    scores = jnp.einsum('nrhgd,nkhd->nhgrk', query_block_rows, key_block, precision=HIGHEST) / jnp.sqrt(jnp.float32(head))
    query_pos = start_index + jnp.arange(token_rows, dtype=jnp.int32)
    key_pos = start_index - margin + jnp.arange(extent, dtype=jnp.int32)
    window = (key_pos[None, :] > query_pos[:, None] - margin) & (key_pos[None, :] <= query_pos[:, None]) & (key_pos[None, :] >= 0)
    distant = (key_pos[None, :] <= query_pos[:, None] - margin) & (key_pos[None, :] >= 0)
    masked = jnp.where(window, scores, jnp.float32(-1e+30))
    summit = lax.optimization_barrier(jnp.max(masked, axis=-1, keepdims=True))
    weights = jnp.where(window, jnp.exp(masked - summit), jnp.float32(0.0))
    linear = jnp.where(distant, jnp.einsum('nrhgf,nkhf->nhgrk', mapped_q, mapped_k, precision=HIGHEST), jnp.float32(0.0))
    damping = jnp.exp(-summit)
    combined = weights + damping * linear
    far_scale = jnp.transpose(damping[..., 0], (0, 3, 1, 2))
    numerator = jnp.einsum('nhgrk,nkhd->nrhgd', combined, value_block, precision=HIGHEST)
    numerator = numerator + far_scale[..., None] * jnp.einsum('nrhgf,nhfd->nrhgd', mapped_q, state, precision=HIGHEST)
    denominator = jnp.transpose(lax.optimization_barrier(jnp.sum(combined, axis=-1)), (0, 3, 1, 2))
    denominator = denominator + far_scale * jnp.einsum('nrhgf,nhf->nrhg', mapped_q, totals, precision=HIGHEST)
    return numerator / denominator[..., None]

def attend_sequence(query_block_rows, key, value, query_feature_map, key_feature_map):
    total = query_block_rows.shape[0]
    token_rows = min(512, total)
    blocks = total // token_rows
    head_group = QUERY_HEAD_COUNT // KEY_VALUE_HEADS
    query_feature_rows = query_feature_map.reshape(KEY_VALUE_HEADS, head_group, HEAD_SIZE, HEAD_SIZE)
    leading_zero_rows = jnp.zeros((WINDOW_KEYS, KEY_VALUE_HEADS * HEAD_SIZE), jnp.float32)
    padded_key_rows = jnp.concatenate([leading_zero_rows, key], axis=0)
    padded_value_rows = jnp.concatenate([leading_zero_rows, value], axis=0)

    def step(carry, index):
        state, totals = carry
        start_index = index * token_rows
        key_block = lax.dynamic_slice_in_dim(padded_key_rows, start_index, token_rows + WINDOW_KEYS, 0).reshape(1, token_rows + WINDOW_KEYS, KEY_VALUE_HEADS, HEAD_SIZE)
        value_block = lax.dynamic_slice_in_dim(padded_value_rows, start_index, token_rows + WINDOW_KEYS, 0).reshape(1, token_rows + WINDOW_KEYS, KEY_VALUE_HEADS, HEAD_SIZE)
        query_block = lax.dynamic_slice_in_dim(query_block_rows, start_index, token_rows, 0).reshape(1, token_rows, KEY_VALUE_HEADS, head_group, HEAD_SIZE)
        result = mix_block(query_block, key_block, value_block, state, totals, query_feature_rows, key_feature_map, start_index)
        key_pos = start_index - WINDOW_KEYS + jnp.arange(token_rows, dtype=jnp.int32)
        present = (key_pos >= 0).astype(jnp.float32)
        mapped = feature_map(jnp.einsum('nkhd,hde->nkhe', key_block[:, :token_rows], key_feature_map, precision=HIGHEST))
        mapped = mapped * present[None, :, None, None]
        state = state + jnp.einsum('nkhf,nkhd->nhfd', mapped, value_block[:, :token_rows], precision=HIGHEST)
        totals = totals + lax.optimization_barrier(jnp.sum(mapped, axis=1))
        return ((state, totals), result.reshape(token_rows, QUERY_HEAD_COUNT * HEAD_SIZE))
    initial_state = (jnp.zeros((1, KEY_VALUE_HEADS, 2 * HEAD_SIZE, HEAD_SIZE), jnp.float32), jnp.zeros((1, KEY_VALUE_HEADS, 2 * HEAD_SIZE), jnp.float32))
    _, outputs = lax.scan(jax.checkpoint(step), initial_state, jnp.arange(blocks, dtype=jnp.int32))
    return outputs.reshape(total, QUERY_HEAD_COUNT * HEAD_SIZE)

def rms_norm(value_block, gain):
    return value_block * lax.rsqrt(lax.optimization_barrier(jnp.mean(value_block * value_block, axis=-1, keepdims=True)) + EPSILON) * gain

def adapted(inputs, weight, down, lift):
    small = low_back(low(matmul(inputs, down)))
    return low_back(low(matmul(inputs, weight) + matmul(small, lift)))

def layer(row, params):
    mixer_gain, query_weight, key_matrix, value_matrix, out_weight, query_down, query_lift, key_down, key_adapter_second, value_down, value_adapter_second, out_down, out_lift, query_feature_map, key_feature_map, ffn_gain, gate_weight, up_weight, down_weight = params
    mixer_in = low(rms_norm(row, mixer_gain))
    query_block_rows = adapted(mixer_in, query_weight, query_down, query_lift)
    key = adapted(mixer_in, key_matrix, key_down, key_adapter_second)
    value = adapted(mixer_in, value_matrix, value_down, value_adapter_second)
    mixed = low_back(low(attend_sequence(query_block_rows, key, value, query_feature_map, key_feature_map)))
    out_low = low_back(low(matmul(mixed, out_down)))
    branch = low_back(matmul(mixed, out_weight) + matmul(out_low, out_lift))
    resid = row + branch
    ffn_in = low(rms_norm(resid, ffn_gain))
    gate = low_back(matmul(ffn_in, gate_weight))
    up = low_back(matmul(ffn_in, up_weight))
    hidden = low(jax.nn.silu(gate) * up)
    return resid + low_back(matmul(hidden, down_weight))

def reference(tokens, lengths, cotangent, mixer_gain, query_weight, key_matrix, value_matrix, out_weight, query_down, query_lift, key_down, key_adapter_second, value_down, value_adapter_second, out_down, out_lift, query_feature_map, key_feature_map, ffn_gain, gate_weight, up_weight, down_weight):
    params = tuple((item.astype(jnp.float32) for item in (mixer_gain, query_weight, key_matrix, value_matrix, out_weight, query_down, query_lift, key_down, key_adapter_second, value_down, value_adapter_second, out_down, out_lift, query_feature_map, key_feature_map, ffn_gain, gate_weight, up_weight, down_weight)))
    inputs = tokens.astype(jnp.float32)
    positions = jnp.arange(LENGTH, dtype=jnp.int32)
    valid = (positions[None, :] < lengths[:, None]).astype(jnp.float32)
    masked_cotangent = cotangent.astype(jnp.float32) * valid[..., None]

    def forward(value_block, weights):
        return lax.map(lambda row: layer(row, weights), value_block)
    result, pull = jax.vjp(forward, inputs, params)
    grad_in, grads = pull(masked_cotangent)
    return (result.astype(jnp.bfloat16), grad_in, grads[0], grads[1], grads[2], grads[3], grads[4], grads[5], grads[6], grads[7], grads[8], grads[9], grads[10], grads[11], grads[12], grads[13], grads[14], grads[15], grads[16], grads[17], grads[18])
```

```python
import functools
import math

import jax
import jax.numpy as jnp
from jax import lax
from jax.experimental import pallas as pl
from jax.experimental.pallas import tpu as pltpu
from jax.sharding import PartitionSpec as P

WINDOW_KEYS = 64


EPSILON = 1e-05
HIGHEST = lax.Precision.HIGHEST
MESH = pl.DeviceIdType.MESH


def plane(seq):
    cores = 2 if seq % 2 == 0 else 1
    chips = seq // cores
    across = max(d for d in range(1, chips + 1) if chips % d == 0 and d * d <= chips)
    return chips // across, across, cores


class Place:
    def __init__(self, seq, mlp):
        self.seq, self.mlp = seq, mlp
        self.ys, self.xs, self.cs = plane(seq)
        self.s, self.m = lax.axis_index("seq"), lax.axis_index("mlp")
        self.c = lax.rem(self.s, self.cs)
        self.x = lax.rem(self.s // self.cs, self.xs)
        self.y = self.s // (self.cs * self.xs)

    def at(self, dy=0, dx=0, dc=0):
        y = lax.rem(self.y + dy + self.ys, self.ys)
        x = lax.rem(self.x + dx + self.xs, self.xs)
        c = lax.rem(self.c + dc + self.cs, self.cs)
        return (y * self.xs + x) * self.cs + c

    def partners(self):
        out = [(None, (self.at(dx=a), self.m)) for a in range(1, self.xs)]
        out += [(None, (self.at(dy=b), self.m)) for b in range(1, self.ys)]
        out += [(None, (self.at(dc=1), self.m))] * (self.cs - 1)
        return out

    def line(self):
        return [(self.m > 0, (self.s, self.m - 1)), (self.m < self.mlp - 1, (self.s, self.m + 1))]


def when(cond, body):
    if cond is None:
        body()
    else:
        pl.when(cond)(body)


def greet(partners):
    barrier = pltpu.get_barrier_semaphore()
    many = jnp.int32(0)
    for cond, device in partners:
        when(
            cond,
            functools.partial(
                pl.semaphore_signal, barrier, inc=1, device_id=device, device_id_type=MESH
            ),
        )
        many = many + (1 if cond is None else cond.astype(jnp.int32))
    pl.semaphore_wait(barrier, many)


class Wire:
    def __init__(self, send, recv):
        self.send, self.recv = send, recv
        self.slots, self.started = {}, []

    def copy(self, key, src, dst, device):
        slot = self.slots.setdefault(key, len(self.slots))
        return pltpu.make_async_remote_copy(
            src_ref=src,
            dst_ref=dst,
            send_sem=self.send.at[slot],
            recv_sem=self.recv.at[slot],
            device_id=device,
            device_id_type=MESH,
        )

    def push(self, cond, key, src, dst, device):
        copy = self.copy(key, src, dst, device)
        when(cond, copy.start)
        self.started.append((cond, copy))

    def pull(self, cond, key, dst, device):
        copy = self.copy(key, dst, dst, device)
        when(cond, copy.wait_recv)

    def drain(self):
        for cond, copy in self.started:
            when(cond, copy.wait_send)
        self.started = []


def both(*conds):
    conds = [cond for cond in conds if cond is not None]
    return functools.reduce(jnp.logical_and, conds) if conds else None


def line_steps(mlp):
    return range(mlp - 1)


def gather_kernel(seq, mlp, weights, lines, *refs):
    count = weights + lines
    ins, outs = refs[:count], refs[count : 2 * count]
    send, recv, local = refs[2 * count :]
    here = Place(seq, mlp)
    wire = Wire(send, recv)
    rows = [ins[k].shape[0] for k in range(weights)]
    cols = [ins[k].shape[1] for k in range(weights)]

    def block(k, s, m, half=None):
        span = pl.ds((s * mlp + m) * rows[k], rows[k])
        tiles = cols[k] // 128
        cut = (tiles // 2 + (k + 1) % 2 * (tiles % 2)) * 128
        if half is None:
            return outs[k].at[span]
        return outs[k].at[span, pl.ds(0, cut) if half == 0 else pl.ds(cut, cols[k] - cut)]

    def strip(k, m):
        depth = ins[k].shape[1]
        return outs[k].at[:, pl.ds(m * depth, depth)]

    def place(k, m):
        return block(k, here.s, m) if k < weights else strip(k, m)

    greet((here.partners() if weights else []) + here.line())
    keep = []
    for k in range(count):
        copy = pltpu.make_async_copy(ins[k], place(k, here.m), local.at[k])
        copy.start()
        keep.append(copy)

    def line_send(k, t):
        for side, step, ok in (
            ("right", 1, both(here.m < mlp - 1, here.m - t >= 0)),
            ("left", -1, both(here.m > 0, here.m + t < mlp)),
        ):
            origin = here.m - step * t
            src = ins[k] if t == 0 else place(k, origin)
            wire.push(ok, ("line", k, side, t), src, place(k, origin), (here.s, here.m + step))

    def line_items(t):
        return (
            ("right", t, here.m - 1 - t, here.m - 1 - t >= 0),
            ("left", t, here.m + 1 + t, here.m + 1 + t < mlp),
        )

    def line_take(k, t):
        for side, t, origin, ok in line_items(t):
            wire.pull(ok, ("line", k, side, t), place(k, origin), (here.s, here.m))

    def to_core(k, item, what, s, half, src=None):
        name, t, origin, ok = item
        if here.cs > 1:
            dst = block(k, s, origin, half)
            wire.push(
                ok, ("core", k, name, t, what), dst if src is None else src, dst, (here.at(dc=1), here.m)
            )

    def spread(k, item):
        name, t, origin, ok = item
        dst = block(k, here.s, origin)
        src = ins[k] if name == "own" else dst
        for a in range(1, here.xs):
            wire.push(ok, ("x", k, name, t, a), src, dst, (here.at(dx=a), here.m))
        for b in range(1, here.ys):
            wire.push(ok, ("y", k, name, t, b), src, dst, (here.at(dy=b), here.m))
        to_core(k, item, "own", here.s, None, src)

    def onward(k, item):
        name, t, origin, ok = item
        for a in range(1, here.xs):
            s = here.at(dx=-a)
            wire.pull(ok, ("x", k, name, t, a), block(k, s, origin), (here.s, here.m))
            for b in range(1, here.ys):
                part = block(k, s, origin, 0)
                wire.push(ok, ("xy", k, name, t, a, b), part, part, (here.at(dy=b), here.m))
            to_core(k, item, ("x", a), s, None)
        for b in range(1, here.ys):
            s = here.at(dy=-b)
            wire.pull(ok, ("y", k, name, t, b), block(k, s, origin), (here.s, here.m))
            for a in range(1, here.xs):
                part = block(k, s, origin, 1)
                wire.push(ok, ("yx", k, name, t, b, a), part, part, (here.at(dx=a), here.m))
            to_core(k, item, ("y", b), s, None)

    def corner(k, item):
        name, t, origin, ok = item
        for a in range(1, here.xs):
            for b in range(1, here.ys):
                s = here.at(dx=-a, dy=-b)
                wire.pull(ok, ("xy", k, name, t, a, b), block(k, s, origin, 0), (here.s, here.m))
                to_core(k, item, ("xy", a, b), s, 0)
                wire.pull(ok, ("yx", k, name, t, b, a), block(k, s, origin, 1), (here.s, here.m))
                to_core(k, item, ("yx", b, a), s, 1)

    def finish(k, item):
        name, t, origin, ok = item
        if here.cs > 1:
            me = (here.s, here.m)
            wire.pull(ok, ("core", k, name, t, "own"), block(k, here.at(dc=1), origin), me)
            for a in range(1, here.xs):
                wire.pull(ok, ("core", k, name, t, ("x", a)), block(k, here.at(dx=-a, dc=1), origin), me)
            for b in range(1, here.ys):
                wire.pull(ok, ("core", k, name, t, ("y", b)), block(k, here.at(dy=-b, dc=1), origin), me)
            for a in range(1, here.xs):
                for b in range(1, here.ys):
                    s = here.at(dx=-a, dy=-b, dc=1)
                    wire.pull(ok, ("core", k, name, t, ("xy", a, b)), block(k, s, origin, 0), me)
                    wire.pull(ok, ("core", k, name, t, ("yx", b, a)), block(k, s, origin, 1), me)

    own = ("own", 0, here.m, None)
    mains, sides = range(weights), range(weights, count)
    groups = [(k, (own,)) for k in mains]
    for k in mains:
        line_send(k, 0)
        spread(k, own)
    for t in line_steps(mlp):
        for k in mains:
            line_take(k, t)
            if t + 1 < mlp - 1:
                line_send(k, t + 1)
            for item in line_items(t):
                spread(k, item)
            groups.append((k, line_items(t)))
    for k in sides:
        line_send(k, 0)
    for step, (k, items) in enumerate(groups):
        for item in items:
            onward(k, item)
        if step % weights == weights - 1 and step // weights < mlp - 1:
            t = step // weights
            for side in sides:
                line_take(side, t)
                if t + 1 < mlp - 1:
                    line_send(side, t + 1)
        if step > 0:
            for item in groups[step - 1][1]:
                corner(groups[step - 1][0], item)
    for k, items in groups[-1:]:
        for item in items:
            corner(k, item)
    for k, items in groups:
        for item in items:
            finish(k, item)
    if not weights:
        for t in line_steps(mlp):
            for side in sides:
                line_take(side, t)
                if t + 1 < mlp - 1:
                    line_send(side, t + 1)
    for copy in keep:
        copy.wait()
    wire.drain()


def gather_all(seq, mlp, weights, lines, ident):
    counts = len(weights) + len(lines)
    ys, xs, cs = plane(seq)
    per_item = (xs - 1) + (ys - 1) + 2 * (xs - 1) * (ys - 1)
    per_item += (cs - 1) * (1 + per_item)
    slots = len(weights) * ((1 + 2 * (mlp - 1)) * per_item) + counts * 2 * (mlp - 1)
    shapes = [jax.ShapeDtypeStruct((seq * mlp * w.shape[0], w.shape[1]), w.dtype) for w in weights]
    shapes += [
        jax.ShapeDtypeStruct((a.shape[0], mlp * a.shape[1], a.shape[2]), a.dtype) for a in lines
    ]
    return pl.pallas_call(
        functools.partial(gather_kernel, seq, mlp, len(weights), len(lines)),
        out_shape=shapes,
        in_specs=[pl.BlockSpec(memory_space=pl.ANY)] * counts,
        out_specs=[pl.BlockSpec(memory_space=pl.ANY)] * counts,
        scratch_shapes=[
            pltpu.SemaphoreType.DMA((slots,)),
            pltpu.SemaphoreType.DMA((slots,)),
            pltpu.SemaphoreType.DMA((counts,)),
        ],
        compiler_params=pltpu.CompilerParams(collective_id=ident, has_side_effects=True),
        name=f"gather_{ident}",
    )(*weights, *lines)


def add_rows(dst, src, extra=()):
    rows = dst.shape[-2]
    step = 16

    @pl.loop(0, rows // step)
    def _(i):
        span = pl.ds(pl.multiple_of(i * step, step), step)
        total = dst[span, :].astype(jnp.float32) + src[span, :].astype(jnp.float32)
        for more in extra:
            total = total + more[span, :].astype(jnp.float32)
        dst[span, :] = total.astype(dst.dtype)


def scatter_kernel(seq, mlp, cuts, small, g_ref, out_ref, *refs):
    if small:
        spread_ref, *refs = refs
    held, from_core, from_first, from_second, from_line, total, send, recv, local, leave = refs
    here = Place(seq, mlp)
    wire = Wire(send, recv)
    ys, xs, cs = here.ys, here.xs, here.cs
    depth = held.shape[3]
    rows = depth // mlp
    me = (here.s, here.m)
    greet(
        here.partners()
        + [(None, (here.s, lax.rem(here.m + j, mlp))) for j in range(1, mlp)]
    )
    chunks = len(cuts) - 1
    span = lambda q: pl.ds(cuts[q], cuts[q + 1] - cuts[q])
    loads = []
    for q in range(chunks):
        loads.append(
            pltpu.make_async_copy(
                g_ref.at[:, :, :, :, span(q)], held.at[:, :, :, :, span(q)], local.at[q]
            )
        )
        loads[-1].start()
    other = lax.rem(here.c + 1, cs)

    def to_core(q):
        loads[q].wait()
        if cs > 1:
            wire.push(
                None,
                ("core", q),
                held.at[:, :, other, :, span(q)],
                from_core.at[:, :, :, span(q)],
                (here.at(dc=1), here.m),
            )

    def first_axis(q):
        return q % 2 == 0

    def mod(v, n):
        return lax.rem(v + n, n)

    def begin(q):
        if cs > 1:
            into = from_core.at[:, :, :, span(q)]
            wire.pull(None, ("core", q), into, me)
            for y in range(ys):
                for x in range(xs):
                    add_rows(held.at[y, x, here.c, :, span(q)], from_core.at[y, x, :, span(q)])
        if first_axis(q):
            for a in range(1, xs):
                wire.push(
                    None,
                    ("first", q, a),
                    held.at[:, mod(here.x + a, xs), here.c, :, span(q)],
                    from_first.at[a - 1, pl.ds(0, ys), :, span(q)],
                    (here.at(dx=a), here.m),
                )
        else:
            for b in range(1, ys):
                wire.push(
                    None,
                    ("first", q, b),
                    held.at[mod(here.y + b, ys), :, here.c, :, span(q)],
                    from_first.at[b - 1, pl.ds(0, xs), :, span(q)],
                    (here.at(dy=b), here.m),
                )

    def middle(q):
        if first_axis(q):
            for a in range(1, xs):
                wire.pull(None, ("first", q, a), from_first.at[a - 1, pl.ds(0, ys), :, span(q)], me)
            if xs > 1:
                for y in range(ys):
                    parts = [from_first.at[a - 1, y, :, span(q)] for a in range(1, xs)]
                    add_rows(held.at[y, here.x, here.c, :, span(q)], parts[0], parts[1:])
            for b in range(1, ys):
                wire.push(
                    None,
                    ("second", q, b),
                    held.at[mod(here.y + b, ys), here.x, here.c, :, span(q)],
                    from_second.at[b - 1, :, span(q)],
                    (here.at(dy=b), here.m),
                )
        else:
            for b in range(1, ys):
                wire.pull(None, ("first", q, b), from_first.at[b - 1, pl.ds(0, xs), :, span(q)], me)
            if ys > 1:
                for x in range(xs):
                    parts = [from_first.at[b - 1, x, :, span(q)] for b in range(1, ys)]
                    add_rows(held.at[here.y, x, here.c, :, span(q)], parts[0], parts[1:])
            for a in range(1, xs):
                wire.push(
                    None,
                    ("second", q, a),
                    held.at[here.y, mod(here.x + a, xs), here.c, :, span(q)],
                    from_second.at[a - 1, :, span(q)],
                    (here.at(dx=a), here.m),
                )

    def last(q):
        many = (ys if first_axis(q) else xs) - 1
        mine = held.at[here.y, here.x, here.c, :, span(q)]
        parts = []
        for b in range(1, many + 1):
            parts.append(from_second.at[b - 1, :, span(q)])
            wire.pull(None, ("second", q, b), parts[-1], me)
        if parts:
            add_rows(mine, parts[0], parts[1:])
        for j in range(1, mlp):
            to = mod(here.m + j, mlp)
            wire.push(
                None,
                ("line", q, j),
                held.at[here.y, here.x, here.c, pl.ds(to * rows, rows), span(q)],
                from_line.at[j - 1, :, span(q)],
                (here.s, to),
            )

    def end(q):
        for j in range(1, mlp):
            wire.pull(None, ("line", q, j), from_line.at[j - 1, :, span(q)], me)
        step = 16

        @pl.loop(0, rows // step)
        def _(i):
            part = pl.ds(pl.multiple_of(i * step, step), step)
            own = pl.ds(pl.multiple_of(here.m * rows + i * step, step), step)
            value = held[here.y, here.x, here.c, own, span(q)].astype(jnp.float32)
            for j in range(1, mlp):
                value = value + from_line[j - 1, part, span(q)].astype(jnp.float32)
            total[part, span(q)] = value

        if small and q == 0:
            share_start()
        else:
            copy = pltpu.make_async_copy(total.at[:, span(q)], out_ref.at[:, span(q)], leave.at[q])
            copy.start()
            leaving.append(copy)

    leaving = []

    def slab(s):
        return spread_ref.at[pl.ds(s * depth, depth)]

    def share_start():
        place = spread_ref.at[pl.ds((here.s * mlp + here.m) * rows, rows)]
        copy = pltpu.make_async_copy(total.at[:, span(0)], place, leave.at[0])
        copy.start()
        leaving.append(copy)
        for j in range(1, mlp):
            wire.push(
                None, ("share", j), total.at[:, span(0)], place, (here.s, lax.rem(here.m + j, mlp))
            )

    def share(step):
        if step == 0:
            leaving[0].wait()
            for j in range(1, mlp):
                origin = lax.rem(here.m - j + mlp, mlp)
                wire.pull(
                    None, ("share", j), spread_ref.at[pl.ds((here.s * mlp + origin) * rows, rows)], me
                )
            for a in range(1, xs):
                wire.push(None, ("sx", a), slab(here.s), slab(here.s), (here.at(dx=a), here.m))
        if step == 1:
            for a in range(1, xs):
                wire.pull(None, ("sx", a), slab(here.at(dx=-a)), me)
            for b in range(1, ys):
                for a in range(xs):
                    s = here.at(dx=-a)
                    wire.push(None, ("sy", a, b), slab(s), slab(s), (here.at(dy=b), here.m))
        if step == 2:
            for b in range(1, ys):
                for a in range(xs):
                    wire.pull(None, ("sy", a, b), slab(here.at(dx=-a, dy=-b)), me)
            if cs > 1:
                for b in range(ys):
                    for a in range(xs):
                        s = here.at(dx=-a, dy=-b)
                        wire.push(None, ("sc", a, b), slab(s), slab(s), (here.at(dc=1), here.m))
        if step == 3 and cs > 1:
            for b in range(ys):
                for a in range(xs):
                    wire.pull(None, ("sc", a, b), slab(here.at(dx=-a, dy=-b, dc=1)), me)

    for q in range(chunks):
        to_core(q)
    for step in range(chunks + 3):
        if step < chunks:
            begin(step)
        if 0 <= step - 1 < chunks:
            middle(step - 1)
        if 0 <= step - 2 < chunks:
            last(step - 2)
        if 0 <= step - 3 < chunks:
            end(step - 3)
        if small and 0 <= step - 4 < 4:
            share(step - 4)
    if small:
        for step in range(max(0, chunks - 1), 4):
            share(step)
    for copy in leaving[1:] if small else leaving:
        copy.wait()
    wire.drain()


def scatter_sum(seq, mlp, grads, pieces, small, ident):
    ys, xs, cs = plane(seq)
    wide = grads.shape[1]
    depth = grads.shape[0] // seq
    rows = depth // mlp
    tiles = wide // 128 - small
    cuts = [128 * (small + tiles * i // pieces) for i in range(pieces + 1)]
    if small:
        cuts = [0] + cuts
    chunks = len(cuts) - 1
    far = max(xs, ys)
    slots = chunks * ((cs - 1) + 2 * (far - 1) + mlp - 1)
    slots += small * (mlp - 1 + xs - 1 + (ys - 1) * xs + ys * xs)
    shapes = [jax.ShapeDtypeStruct((rows, wide), jnp.float32)]
    if small:
        shapes.append(jax.ShapeDtypeStruct((grads.shape[0], 128), jnp.float32))
    kind = grads.dtype
    used = wide * depth * kind.itemsize
    vmem = used * (seq + seq // cs + (far - 1) * far + far - 1 + 1) + 3 * rows * wide * 4
    return pl.pallas_call(
        functools.partial(scatter_kernel, seq, mlp, cuts, small),
        out_shape=shapes,
        in_specs=[pl.BlockSpec(memory_space=pl.ANY)],
        out_specs=[pl.BlockSpec(memory_space=pl.ANY)] * len(shapes),
        scratch_shapes=[
            pltpu.VMEM((ys, xs, cs, depth, wide), kind),
            pltpu.VMEM((ys, xs, depth, wide), kind),
            pltpu.VMEM((max(far - 1, 1), far, depth, wide), kind),
            pltpu.VMEM((max(far - 1, 1), depth, wide), kind),
            pltpu.VMEM((max(mlp - 1, 1), rows, wide), kind),
            pltpu.VMEM((rows, wide), jnp.float32),
            pltpu.SemaphoreType.DMA((slots,)),
            pltpu.SemaphoreType.DMA((slots,)),
            pltpu.SemaphoreType.DMA((chunks,)),
            pltpu.SemaphoreType.DMA((chunks,)),
        ],
        compiler_params=pltpu.CompilerParams(
            collective_id=ident, has_side_effects=True, vmem_limit_bytes=min(vmem + 4 * 2**20, 60 * 2**20)
        ),
        name=f"scatter_{ident}",
    )(grads.reshape(ys, xs, cs, depth, wide))


def from_behind(value, axis, steps):
    count = lax.axis_size(axis)
    initial, last = (max(0, -steps), min(count, count - steps))
    return lax.ppermute(value, axis, [(source, source + steps) for source in range(initial, last)])


def flat_rows(parts, count, kind):
    flat = jnp.concatenate([part.astype(kind).reshape(-1) for part in parts])
    unit = count * 16 * 128
    padded = -(-flat.shape[0] // unit) * unit
    return jnp.pad(flat, (0, padded - flat.shape[0])).reshape(-1, 128)


def unflat(rows, parts):
    flat = rows.reshape(-1)
    pieces, place = [], 0
    for part in parts:
        pieces.append(flat[place : place + part.size].reshape(part.shape))
        place += part.size
    return tuple(pieces)


def scan_devices(parts, axes, later):
    count = lax.axis_size(axes)
    rows = flat_rows(parts, count, jnp.bfloat16)
    seen = lax.all_to_all(rows, axes, 0, 0, tiled=True).astype(jnp.float32)
    seen = seen.reshape(count, -1, 128)
    order = jnp.arange(count)
    pick = order[:, None] < order[None, :] if later else order[:, None] > order[None, :]
    sums = jnp.einsum("ds,srl->drl", pick.astype(jnp.float32), seen, precision=HIGHEST)
    back = lax.all_to_all(sums.reshape(rows.shape), axes, 0, 0, tiled=True)
    return unflat(back, parts)


def pad_cols(parts, width):
    have = sum(part.shape[1] for part in parts)
    return jnp.concatenate(
        list(parts) + [jnp.zeros((parts[0].shape[0], width - have), parts[0].dtype)], axis=1
    )


AUG = 16
FAR_BELOW = -1e30


def mm(left, right):
    return lax.dot_general(left, right, (((1,), (0,)), ((), ())), preferred_element_type=jnp.float32)


def mm_tn(left, right):
    return lax.dot_general(left, right, (((0,), (0,)), ((), ())), preferred_element_type=jnp.float32)


def mm_nt(left, right):
    return lax.dot_general(left, right, (((1,), (1,)), ((), ())), preferred_element_type=jnp.float32)


def half(value):
    return value.astype(jnp.bfloat16)


def soft_pair(lifted):
    high = jnp.exp(lifted - jnp.max(lifted, axis=0, keepdims=True))
    low = jnp.exp(jnp.min(lifted, axis=0, keepdims=True) - lifted)
    high = high * (1.0 / jnp.sum(high, axis=0, keepdims=True))
    low = low * (1.0 / jnp.sum(low, axis=0, keepdims=True))
    return high, low


def soft_pair_back(high, low, grad):
    d = high.shape[0]
    gh, gl = grad[:d], grad[d:]
    return high * (gh - jnp.sum(high * gh, axis=0, keepdims=True)) - low * (
        gl - jnp.sum(low * gl, axis=0, keepdims=True)
    )


def with_ones(values):
    ones = lax.broadcasted_iota(jnp.int32, (AUG, values.shape[1]), 0) == 0
    return jnp.concatenate([values, jnp.where(ones, 1.0, 0.0).astype(values.dtype)], axis=0)


def key_features(key_t, map_ref):
    return soft_pair(mm_tn(map_ref[0], key_t))


def own_state_kernel(key_ref, value_ref, map_ref, out_ref):
    high, low = key_features(key_ref[...], map_ref)
    mapped = half(jnp.concatenate([high, low], axis=0))
    out_ref[0] = half(mm_nt(with_ones(value_ref[...]), mapped))


def lanes_joined(ref, group):
    d = ref.shape[0] // group
    return jnp.concatenate([ref[g * d : (g + 1) * d, :] for g in range(group)], axis=1)


class Mix:
    def __init__(self, group, first, query_ref, key_ref, value_ref, tail_k, tail_v, qmap_ref, kmap_ref, prior_ref):
        self.present = jnp.where(first, jnp.float32(0.0), jnp.float32(1.0))
        self.query = lanes_joined(query_ref, group)
        self.key, self.value = key_ref[...], value_ref[...]
        self.tail_key, self.tail_value = tail_k[0, 0], tail_v[0, 0]
        d, rows = self.key.shape
        keep = self.tail_key.shape[1]
        scale = 1.0 / math.sqrt(d)
        lifted = jnp.concatenate(
            [mm_tn(qmap_ref[g], self.query[:, g * rows : (g + 1) * rows]) for g in range(group)], axis=1
        )
        self.q_high, self.q_low = soft_pair(lifted)
        self.mapped_q = half(jnp.concatenate([self.q_high, self.q_low], axis=0))
        self.k_high, self.k_low = key_features(self.key, kmap_ref)
        self.t_high, self.t_low = key_features(self.tail_key, kmap_ref)
        self.mapped_k = half(jnp.concatenate([self.k_high, self.k_low], axis=0))
        self.mapped_t = half(jnp.concatenate([self.t_high, self.t_low], axis=0) * self.present)
        self.value_aug, self.tail_aug = with_ones(self.value), with_ones(self.tail_value)
        self.state = half(prior_ref[0].astype(jnp.float32) - mm_nt(self.tail_aug, self.mapped_t))
        wide = group * rows
        a = lax.broadcasted_iota(jnp.int32, (rows, wide), 0)
        r = lax.rem(lax.broadcasted_iota(jnp.int32, (rows, wide), 1), rows)
        self.far = a <= r - keep
        near = (a <= r) & (a > r - keep)
        t = lax.broadcasted_iota(jnp.int32, (keep, wide), 0)
        r = lax.rem(lax.broadcasted_iota(jnp.int32, (keep, wide), 1), rows)
        here = jnp.logical_not(first)
        self.tail_far = (t <= r) & here
        tail_near = (t > r) & here
        scores = jnp.where(near, mm_tn(self.key, self.query) * scale, FAR_BELOW)
        tail_scores = jnp.where(tail_near, mm_tn(self.tail_key, self.query) * scale, FAR_BELOW)
        summit = jnp.maximum(
            jnp.max(scores, axis=0, keepdims=True), jnp.max(tail_scores, axis=0, keepdims=True)
        )
        self.damping = jnp.exp(-summit)
        self.weights = jnp.where(near, jnp.exp(scores - summit), 0.0)
        self.tail_weights = jnp.where(tail_near, jnp.exp(tail_scores - summit), 0.0)
        self.combined = self.weights + jnp.where(
            self.far, self.damping * mm_tn(self.mapped_k, self.mapped_q), 0.0
        )
        self.tail_combined = self.tail_weights + jnp.where(
            self.tail_far, self.damping * mm_tn(self.mapped_t, self.mapped_q), 0.0
        )
        self.scale = scale


def mix_kernel(
    group, seq_mlp, query_ref, key_ref, value_ref, tail_k, tail_v, qmap_ref, kmap_ref, prior_ref,
    mixed_ref, attended_ref, total_ref,
):
    first = lax.axis_index(seq_mlp) == 0
    mix = Mix(group, first, query_ref, key_ref, value_ref, tail_k, tail_v, qmap_ref, kmap_ref, prior_ref)
    d, rows = mix.key.shape
    summed = mm(mix.value_aug, half(mix.combined)) + mm(mix.tail_aug, half(mix.tail_combined))
    summed = summed + mix.damping * mm(mix.state, mix.mapped_q)
    total = summed[d : d + 1]
    attended = summed[:d] / total
    total_ref[0] = total
    for g in range(group):
        part = attended[:, g * rows : (g + 1) * rows]
        mixed_ref[g * d : (g + 1) * d, :] = half(part)
        attended_ref[g * d : (g + 1) * d, :] = part


def mix_back_kernel(
    group, seq_mlp, query_ref, key_ref, value_ref, tail_k, tail_v, qmap_ref, kmap_ref, prior_ref,
    attended_ref, total_ref, grad_ref,
    dq_ref, dk_ref, dv_ref, dmap_ref, state_ref, tail_dk, tail_dv, dqmap_ref, dkmap_ref,
):
    first = lax.axis_index(seq_mlp) == 0
    mix = Mix(group, first, query_ref, key_ref, value_ref, tail_k, tail_v, qmap_ref, kmap_ref, prior_ref)
    d, rows = mix.key.shape
    scale = mix.scale
    grad = lanes_joined(grad_ref, group)
    attended = lanes_joined(attended_ref, group)
    inverse = 1.0 / total_ref[0]
    grad_wide = grad.astype(jnp.float32)
    mean = jnp.sum(grad_wide * attended, axis=0, keepdims=True)
    dweight = (mm_tn(mix.value, grad) - mean) * inverse
    tail_dweight = (mm_tn(mix.tail_value, grad) - mean) * inverse
    ds, tail_ds = half(mix.weights * dweight), half(mix.tail_weights * tail_dweight)
    dfar = half(jnp.where(mix.far, mix.damping * dweight, 0.0))
    tail_dfar = half(jnp.where(mix.tail_far, mix.damping * tail_dweight, 0.0))
    dv_ref[0] = mm_nt(grad, half(mix.combined * inverse))
    tail_value_grad = mm_nt(grad, half(mix.tail_combined * inverse))
    dquery = (mm(mix.key, ds) + mm(mix.tail_key, tail_ds)) * scale
    dk_ref[0] = mm_nt(mix.query, ds) * scale
    tail_key_grad = mm_nt(mix.query, tail_ds) * scale
    row = lax.broadcasted_iota(jnp.int32, (AUG, grad.shape[1]), 0) == 0
    daug = jnp.concatenate([grad_wide * inverse, jnp.where(row, -mean * inverse, 0.0)], axis=0)
    daug = half(daug * mix.damping)
    dmapped_q = mm(mix.mapped_k, dfar) + mm(mix.mapped_t, tail_dfar) + mm_tn(mix.state, daug)
    dmap_ref[0] = mm_nt(mix.mapped_q, dfar)
    dstate = mm_nt(daug, mix.mapped_q)
    state_ref[0] = half(dstate)
    own = half(dstate)
    tail_dmap = mm_nt(mix.mapped_q, tail_dfar) - mm_tn(own, mix.tail_aug)
    tail_value_grad = tail_value_grad - mm(own[:d], mix.mapped_t)
    dlifted = half(soft_pair_back(mix.q_high, mix.q_low, dmapped_q))
    starting = pl.program_id(1) == 0
    for g in range(group):
        lanes = slice(g * rows, (g + 1) * rows)
        part = dlifted[:, lanes]
        dq_ref[g * d : (g + 1) * d, :] = half(dquery[:, lanes] + mm(qmap_ref[g], part))
        weight = mm_nt(mix.query[:, lanes], part)
        dqmap_ref[g] = jnp.where(starting, weight, weight + dqmap_ref[g])
    tail_lifted = half(soft_pair_back(mix.t_high, mix.t_low, tail_dmap) * mix.present)
    tail_dk[0, 0] = half((tail_key_grad + mm(kmap_ref[0], tail_lifted)) * mix.present)
    tail_dv[0, 0] = half(tail_value_grad * mix.present)
    weight = mm_nt(mix.tail_key, tail_lifted)
    dkmap_ref[0] = jnp.where(starting, weight, weight + dkmap_ref[0])


def key_back_kernel(
    key_ref, value_ref, kmap_ref, later_ref, dmap_ref, dk_in, dv_in, back_k, back_v,
    dk_ref, dv_ref, dkmap_ref,
):
    key, value = key_ref[...], value_ref[...]
    d, rows = key.shape
    keep = back_k.shape[3]
    high, low = key_features(key, kmap_ref)
    mapped = half(jnp.concatenate([high, low], axis=0))
    later = half(later_ref[0])
    dmap = dmap_ref[0] + mm_tn(later, with_ones(value))
    dlifted = half(soft_pair_back(high, low, dmap))
    dkey = dk_in[0] + mm(kmap_ref[0], dlifted)
    dvalue = dv_in[0] + mm(later[:d], mapped)
    front = jnp.zeros((d, rows - keep), jnp.float32)
    dk_ref[...] = half(dkey + jnp.concatenate([front, back_k[0, 0].astype(jnp.float32)], axis=1))
    dv_ref[...] = half(dvalue + jnp.concatenate([front, back_v[0, 0].astype(jnp.float32)], axis=1))
    weight = mm_nt(key, dlifted)
    starting = pl.program_id(1) == 0
    dkmap_ref[0] = jnp.where(starting, weight, weight + dkmap_ref[0])


class Attention:
    def __init__(self, batch, local, heads, group, d, keep):
        self.batch, self.local, self.heads, self.group, self.d, self.keep = batch, local, heads, group, d, keep
        self.grid = (heads, batch)
        width = heads * group
        block = pl.BlockSpec
        self.query = block((group * d, local), lambda h, n: (h, n))
        self.key = block((d, local), lambda h, n: (width + h, n))
        self.value = block((d, local), lambda h, n: (width + heads + h, n))
        self.tail_k = block((1, 1, d, keep), lambda h, n: (n, h, 0, 0))
        self.tail_v = block((1, 1, d, keep), lambda h, n: (n, heads + h, 0, 0))
        self.qmap = block((group, d, d), lambda h, n: (h, 0, 0))
        self.kmap = block((1, d, d), lambda h, n: (h, 0, 0))
        self.state = block((1, d + AUG, 2 * d), lambda h, n: (n * heads + h, 0, 0))
        self.total = block((1, 1, group * local), lambda h, n: (n * heads + h, 0, 0))
        self.own = block((1, d, local), lambda h, n: (n * heads + h, 0, 0))
        self.dmap = block((1, 2 * d, local), lambda h, n: (n * heads + h, 0, 0))
        self.out_kv = block((d, local), lambda h, n: (h, n))

    def call(self, kernel, ins, outs, shapes, name, *args):
        return pl.pallas_call(
            kernel,
            grid=self.grid,
            in_specs=ins,
            out_specs=outs,
            out_shape=shapes,
            compiler_params=pltpu.CompilerParams(vmem_limit_bytes=48 * 2**20),
            name=name,
        )(*args)

    def shape(self, dims, kind=jnp.float32):
        return jax.ShapeDtypeStruct(dims, kind)

    def own_state(self, qkv, kmap):
        pairs = self.batch * self.heads
        return self.call(
            own_state_kernel,
            [self.key, self.value, self.kmap],
            self.state,
            self.shape((pairs, self.d + AUG, 2 * self.d), jnp.bfloat16),
            "own_state",
            qkv, qkv, kmap,
        )

    def mixed(self, qkv, tails, qmap, kmap, prior):
        wide = self.heads * self.group * self.d
        tokens = self.batch * self.local
        return self.call(
            functools.partial(mix_kernel, self.group, ("seq", "mlp")),
            [self.query, self.key, self.value, self.tail_k, self.tail_v, self.qmap, self.kmap, self.state],
            [self.query, self.query, self.total],
            [
                self.shape((wide, tokens), jnp.bfloat16),
                self.shape((wide, tokens)),
                self.shape((self.batch * self.heads, 1, self.group * self.local)),
            ],
            "mix",
            qkv, qkv, qkv, tails, tails, qmap, kmap, prior,
        )

    def back(self, qkv, tails, qmap, kmap, prior, attended, total, grad):
        wide = self.heads * self.group * self.d
        tokens = self.batch * self.local
        pairs = self.batch * self.heads
        tail = self.shape((self.batch, self.heads, self.d, self.keep), jnp.bfloat16)
        return self.call(
            functools.partial(mix_back_kernel, self.group, ("seq", "mlp")),
            [self.query, self.key, self.value, self.tail_k, self.tail_v, self.qmap, self.kmap, self.state]
            + [self.query, self.total, self.query],
            [self.query, self.own, self.own, self.dmap, self.state, self.tail_k, self.tail_k, self.qmap, self.kmap],
            [
                self.shape((wide, tokens), jnp.bfloat16),
                self.shape((pairs, self.d, self.local)),
                self.shape((pairs, self.d, self.local)),
                self.shape((pairs, 2 * self.d, self.local)),
                self.shape((pairs, self.d + AUG, 2 * self.d), jnp.bfloat16),
                tail,
                tail,
                self.shape((self.heads * self.group, self.d, self.d)),
                self.shape((self.heads, self.d, self.d)),
            ],
            "mix_back",
            qkv, qkv, qkv, tails, tails, qmap, kmap, prior, attended, total, grad,
        )

    def key_back(self, qkv, kmap, later, dmap, dk, dv, back_k, back_v):
        tokens = self.batch * self.local
        kv = self.shape((self.heads * self.d, tokens), jnp.bfloat16)
        return self.call(
            key_back_kernel,
            [self.key, self.value, self.kmap, self.state, self.dmap, self.own, self.own, self.tail_k, self.tail_k],
            [self.out_kv, self.out_kv, self.kmap],
            [kv, kv, self.shape((self.heads, self.d, self.d))],
            "key_back",
            qkv, qkv, kmap, later, dmap, dk, dv, back_k, back_v,
        )


def product(left, right):
    return jnp.dot(left, right, preferred_element_type=jnp.float32)


def contract_rows(left, right):
    return lax.dot_general(
        left, right, (((0,), (0,)), ((), ())), preferred_element_type=jnp.float32
    )


def contract_down(left, right):
    return lax.dot_general(
        left, right, (((0,), (1,)), ((), ())), preferred_element_type=jnp.float32
    )


def contract_cols(left, right):
    return lax.dot_general(
        left, right, (((1,), (1,)), ((), ())), preferred_element_type=jnp.float32
    )


def shards(
    tokens,
    lengths,
    cotangent,
    mixer_gain,
    query_weight,
    key_matrix,
    value_matrix,
    out_weight,
    query_down,
    query_lift,
    key_down,
    key_adapter_second,
    value_down,
    value_adapter_second,
    out_down,
    out_lift,
    query_feature_map,
    key_feature_map,
    ffn_gain,
    gate_weight,
    up_weight,
    down_weight,
):
    batch, local, width = tokens.shape
    count = batch * local
    start_index = lax.axis_index(("seq", "mlp")) * local
    q_width, kv_width, rank = query_weight.shape[1], key_matrix.shape[1], query_down.shape[1]
    wide = q_width + 2 * kv_width
    lanes = -(-3 * rank // 128) * 128
    positions = start_index + jnp.arange(local, dtype=jnp.int32)
    live = positions[None, :] < lengths[:, None]
    grad_out = jnp.where(live[..., None], cotangent, jnp.zeros_like(cotangent))
    seq, mlp = lax.axis_size("seq"), lax.axis_size("mlp")
    full_qkv, full_out, grad_rows = gather_all(
        seq,
        mlp,
        [
            pad_cols(
                (query_weight, key_matrix, value_matrix, query_down, key_down, value_down), wide + lanes
            ),
            pad_cols((out_weight, out_down), out_weight.shape[1] + lanes),
        ],
        [grad_out],
        1,
    )
    full_qkv, gate_weight, up_weight, down_weight = lax.optimization_barrier(
        (full_qkv, gate_weight, up_weight, down_weight)
    )
    part_gate, part_up, part_down = (
        lax.all_gather(gate_weight, "seq", axis=0, tiled=True),
        lax.all_gather(up_weight, "seq", axis=0, tiled=True),
        lax.all_gather(down_weight, "seq", axis=1, tiled=True),
    )
    lift_qkv = jnp.zeros((lanes, wide), jnp.bfloat16)
    lift_qkv = lift_qkv.at[:rank, :q_width].set(query_lift)
    lift_qkv = lift_qkv.at[rank : 2 * rank, q_width : q_width + kv_width].set(key_adapter_second)
    lift_qkv = lift_qkv.at[2 * rank : 3 * rank, q_width + kv_width :].set(value_adapter_second)
    lift_out = jnp.zeros((lanes, width), jnp.bfloat16).at[:rank].set(out_lift)
    base = tokens.astype(jnp.float32).reshape(count, width)
    gain_mixer = mixer_gain.astype(jnp.float32)
    scale_mixer = lax.rsqrt(jnp.mean(base * base, axis=-1, keepdims=True) + EPSILON)
    mixer_in = (base * scale_mixer * gain_mixer).astype(jnp.bfloat16)
    projected = contract_down(full_qkv, mixer_in)
    qkv_low = projected[wide:].astype(jnp.bfloat16)
    qkv = (projected[:wide] + contract_rows(lift_qkv, qkv_low)).astype(jnp.bfloat16)
    key_heads = key_feature_map.shape[0]
    head = key_feature_map.shape[1]
    head_group = query_feature_map.shape[0] // key_heads
    attention = Attention(batch, local, key_heads, head_group, head, WINDOW_KEYS)
    own_tails = qkv[q_width:].reshape(2 * key_heads, head, batch, local)[..., local - WINDOW_KEYS :]
    tails = from_behind(jnp.transpose(own_tails, (2, 0, 1, 3)), ("seq", "mlp"), 1)
    own_state = attention.own_state(qkv, key_feature_map)
    (prior,) = scan_devices((own_state,), ("seq", "mlp"), False)
    mixed, attended, totals = attention.mixed(qkv, tails, query_feature_map, key_feature_map, prior)
    out_both = contract_rows(mixed, full_out)
    out_low = out_both[:, width:].astype(jnp.bfloat16)
    branch = out_both[:, :width] + product(out_low, lift_out)
    resid = base + branch
    gain_ffn = ffn_gain.astype(jnp.float32)
    scale_ffn = lax.rsqrt(jnp.mean(resid * resid, axis=-1, keepdims=True) + EPSILON)
    ffn_in = (resid * scale_ffn * gain_ffn).astype(jnp.bfloat16)
    (gathered,) = gather_all(seq, mlp, [], [ffn_in.reshape(batch, local, width)], 2)
    gathered = gathered.reshape(-1, width)
    grad_rows = grad_rows.reshape(-1, width)
    gate = product(gathered, part_gate)
    up = product(gathered, part_up)
    sigma = jax.nn.sigmoid(gate)
    active = gate * sigma
    hidden = (active * up).astype(jnp.bfloat16)
    partial_value = product(hidden, part_down).reshape(batch, -1, width)
    ffn_out = lax.psum_scatter(
        partial_value.astype(jnp.bfloat16), "mlp", scatter_dimension=1, tiled=True
    ).astype(jnp.float32)
    layer_output = (resid.reshape(batch, local, width) + ffn_out).astype(jnp.bfloat16)
    grad_hidden = contract_cols(grad_rows, part_down)
    grad_down = contract_rows(hidden, grad_rows)
    grad_gate = (grad_hidden * up * sigma * (1.0 + gate * (1.0 - sigma))).astype(jnp.bfloat16)
    grad_up = (grad_hidden * active).astype(jnp.bfloat16)
    grad_gate_weight = contract_rows(gathered, grad_gate)
    grad_up_weight = contract_rows(gathered, grad_up)
    grad_ffn_part = contract_cols(grad_gate, part_gate) + contract_cols(grad_up, part_up)
    grad_ffn = (
        lax.psum_scatter(
            grad_ffn_part.reshape(batch, -1, width).astype(jnp.bfloat16),
            "mlp",
            scatter_dimension=1,
            tiled=True,
        )
        .astype(jnp.float32)
        .reshape(count, width)
    )
    grad_ffn_gain = jnp.sum(grad_ffn * resid * scale_ffn, axis=0)
    scaled_ffn = grad_ffn * gain_ffn
    grad_resid = (
        grad_out.astype(jnp.float32).reshape(count, width)
        + scale_ffn * scaled_ffn
        - resid * scale_ffn**3 * jnp.mean(scaled_ffn * resid, axis=-1, keepdims=True)
    )
    grad_branch = grad_resid.astype(jnp.bfloat16)
    grad_out_low = contract_cols(grad_branch, lift_out).astype(jnp.bfloat16)
    grad_out_lift = contract_rows(out_low, grad_branch)[:rank]
    grad_out_both = jnp.concatenate([grad_branch, grad_out_low], axis=1)
    grad_mixed = contract_cols(full_out, grad_out_both).astype(jnp.bfloat16)
    (
        grad_queries,
        key_part,
        value_part,
        map_part,
        grad_state,
        tail_keys,
        tail_values,
        grad_feature_q,
        tail_feature_k,
    ) = attention.back(
        qkv, tails, query_feature_map, key_feature_map, prior, attended, totals, grad_mixed
    )
    (later,) = scan_devices((grad_state,), ("seq", "mlp"), True)
    back_keys, back_values = from_behind((tail_keys, tail_values), ("seq", "mlp"), -1)
    grad_keys, grad_values, own_feature_k = attention.key_back(
        qkv, key_feature_map, later, map_part, key_part, value_part, back_keys, back_values
    )
    grad_feature_key = tail_feature_k + own_feature_k
    grad_qkv = jnp.concatenate([grad_queries, grad_keys, grad_values], axis=0)
    grad_qkv_low = product(lift_qkv, grad_qkv).astype(jnp.bfloat16)
    grad_lifts = contract_cols(qkv_low[: 3 * rank], grad_qkv)
    grad_query_lift = grad_lifts[:rank, :q_width]
    grad_key_lift = grad_lifts[rank : 2 * rank, q_width : q_width + kv_width]
    grad_value_lift = grad_lifts[2 * rank :, q_width + kv_width :]
    grad_qkv_both = jnp.concatenate([grad_qkv, grad_qkv_low], axis=0)
    grad_mixer = contract_down(grad_qkv_both, full_qkv)
    grad_mixer_gain = jnp.sum(grad_mixer * base * scale_mixer, axis=0)
    scaled_mixer = grad_mixer * gain_mixer
    grad_tokens = (
        grad_resid
        + scale_mixer * scaled_mixer
        - base * scale_mixer**3 * jnp.mean(scaled_mixer * base, axis=-1, keepdims=True)
    )
    smalls = (
        grad_query_lift,
        grad_key_lift,
        grad_value_lift,
        grad_out_lift,
        grad_feature_q.reshape(query_feature_map.shape),
        grad_feature_key,
        grad_mixer_gain,
        grad_ffn_gain,
    )
    flat = jnp.concatenate([part.astype(jnp.bfloat16).reshape(-1) for part in smalls])
    flat = jnp.pad(flat, (0, width * 128 - flat.shape[0])).reshape(width, 128)
    packed = jnp.concatenate(
        [
            flat,
            contract_down(mixer_in, grad_qkv_both).astype(jnp.bfloat16),
            product(mixed, grad_out_both).astype(jnp.bfloat16),
        ],
        axis=1,
    )
    sums, spread = scatter_sum(seq, mlp, packed, 6, 1, 3)
    sum_qkv, sum_out = sums[:, 128 : 128 + wide + lanes], sums[:, 128 + wide + lanes :]
    (
        sum_query_lift,
        sum_key_lift,
        sum_value_lift,
        sum_out_lift,
        sum_feature_query,
        sum_feature_key,
        sum_mixer_gain,
        sum_ffn_gain,
    ) = unflat(spread, smalls)
    sum_query_weight = sum_qkv[:, :q_width]
    sum_key_weight = sum_qkv[:, q_width : q_width + kv_width]
    sum_value_weight = sum_qkv[:, q_width + kv_width : wide]
    sum_query_down, sum_key_down, sum_value_down = (
        sum_qkv[:, wide + part * rank : wide + (part + 1) * rank] for part in range(3)
    )
    sum_out_weight = sum_out[:, :width]
    sum_out_down = sum_out[:, width : width + rank]
    sum_gate, sum_up, sum_down = (
        lax.psum_scatter(
            grad_gate_weight.astype(jnp.bfloat16), "seq", scatter_dimension=0, tiled=True
        ).astype(jnp.float32),
        lax.psum_scatter(
            grad_up_weight.astype(jnp.bfloat16), "seq", scatter_dimension=0, tiled=True
        ).astype(jnp.float32),
        lax.psum_scatter(
            grad_down.astype(jnp.bfloat16), "seq", scatter_dimension=1, tiled=True
        ).astype(jnp.float32),
    )
    return (
        layer_output,
        grad_tokens.reshape(batch, local, width),
        sum_mixer_gain,
        sum_query_weight,
        sum_key_weight,
        sum_value_weight,
        sum_out_weight,
        sum_query_down,
        sum_query_lift,
        sum_key_down,
        sum_key_lift,
        sum_value_down,
        sum_value_lift,
        sum_out_down,
        sum_out_lift,
        sum_feature_query,
        sum_feature_key,
        sum_ffn_gain,
        sum_gate,
        sum_up,
        sum_down,
    )


def solution(mesh):
    in_specs = (
        P(None, ("seq", "mlp"), None),
        P(),
        P(None, ("seq", "mlp"), None),
        P(),
        P(("seq", "mlp"), None),
        P(("seq", "mlp"), None),
        P(("seq", "mlp"), None),
        P(("seq", "mlp"), None),
        P(("seq", "mlp"), None),
        P(),
        P(("seq", "mlp"), None),
        P(),
        P(("seq", "mlp"), None),
        P(),
        P(("seq", "mlp"), None),
        P(),
        P(),
        P(),
        P(),
        P("seq", "mlp"),
        P("seq", "mlp"),
        P("mlp", "seq"),
    )
    out_specs = (
        P(None, ("seq", "mlp"), None),
        P(None, ("seq", "mlp"), None),
        P(),
        P(("seq", "mlp"), None),
        P(("seq", "mlp"), None),
        P(("seq", "mlp"), None),
        P(("seq", "mlp"), None),
        P(("seq", "mlp"), None),
        P(),
        P(("seq", "mlp"), None),
        P(),
        P(("seq", "mlp"), None),
        P(),
        P(("seq", "mlp"), None),
        P(),
        P(),
        P(),
        P(),
        P("seq", "mlp"),
        P("seq", "mlp"),
        P("mlp", "seq"),
    )
    return jax.shard_map(shards, mesh=mesh, in_specs=in_specs, out_specs=out_specs, check_vma=False)
```
